32 devices in a mesh: row: 8 (over z, y), col: 4 (over x, core).
Axes of the slice: x: 2, y: 2, z: 4, core: 2. Of those that a mesh axis runs over, the one named last changes fastest.
Arguments:
- sources: float32 [16384, 256], P(('row', 'col')), may hold values from -6 to 6
- level_factors: float32 [8, 128, 2, 128, 128], P(None, ('row', 'col')), may hold values from -0.375 to 0.375
Outputs:
- fields: float32 [4096, 256], P(('row', 'col'))
The draws below stay inside these ranges and needn't reach their ends.
All inputs are finite; a program needn't handle non-finite values.
Results may differ from the reference program's by a relative error of at most 0.00012.
Values sent between devices are 32-bit elements; how exact they have to be, the bound alone decides.
A program may use at most 64 MiB of HBM per device.

```python
import jax
import jax.numpy as jnp
from jax import lax

BLOCK = 128
BPD = 4
RHS = 256
ROW_LEVELS = 5
COL_LEVELS = 3
NB = 128
UNKNOWNS = 16384
N_ROW = 8
N_COL = 4


def level_of(stream_key, shape, split, low, high):
    factor_of, own = 1.0, jax.random.fold_in(stream_key, 6)
    for position, shards_of in split:
        steps = jnp.exp(jax.random.uniform(jax.random.fold_in(own, position), (shards_of,), jnp.float32, low / len(split), high / len(split)))
        factor_of = factor_of * jnp.repeat(steps, shape[position] // shards_of).reshape([-1 if axis == position else 1 for axis in range(len(shape))])
    return factor_of


def centred(rng, dims, deviation, reach, shards=(), kind=jnp.bfloat16):
    values = deviation * jax.random.normal(rng, dims, jnp.float32)
    if shards:
        values = values * level_of(rng, dims, shards, -0.22, 0.18)
    return jnp.clip(values, -reach, reach).astype(kind)


def setup_inputs(seed: int = 0) -> dict:
    seeds = jax.random.split(jax.random.key(seed), 3)
    sources = centred(seeds[0], (UNKNOWNS, RHS), 1.0, 6.0, ((0, 32),), jnp.float32)
    level_factors = centred(seeds[1], (ROW_LEVELS + COL_LEVELS, NB, 2, BLOCK, BLOCK), (2 * BLOCK) ** -0.5, 0.375, ((1, 32),), jnp.float32)
    return dict(sources=sources, level_factors=level_factors)


def reference(sources, level_factors):
    state = sources.reshape(NB, BLOCK, RHS)
    log_row = N_ROW.bit_length() - 1
    log_col = N_COL.bit_length() - 1
    block_ids = jnp.arange(NB, dtype=jnp.int32)
    for level in range(ROW_LEVELS + COL_LEVELS):
        if level < ROW_LEVELS:
            stride = N_COL << (level % log_row)
        else:
            stride = 1 << ((level - ROW_LEVELS) % log_col)
        partner = state[block_ids ^ (stride * BPD)]
        factors = level_factors[level]
        state = jnp.einsum("bij,bjr->bir", factors[:, 0], state, precision=lax.Precision.HIGHEST) + jnp.einsum("bij,bjr->bir", factors[:, 1], partner, precision=lax.Precision.HIGHEST)
    panels = state.reshape(N_ROW, N_COL, BPD * BLOCK, RHS)
    return jnp.sum(panels, axis=1).reshape(N_ROW * BPD * BLOCK, RHS)
```

```python
import functools

import jax
import jax.numpy as jnp
from jax import lax
from jax.experimental import pallas as pl
from jax.experimental.pallas import tpu as pltpu
from jax.sharding import PartitionSpec as P

ROW_LEVELS = 5
COL_LEVELS = 3
HALVES = 2
MESH = pl.DeviceIdType.MESH


def flip(index, mask):
    bit = 1
    while bit <= mask:
        if mask & bit:
            index = index + bit * (1 - 2 * ((index // bit) % 2))
        bit *= 2
    return index


def dot(a, b):
    return jnp.dot(a, b, precision=lax.Precision.HIGHEST, preferred_element_type=jnp.float32)


def schedule(blocks):
    order = sorted(range(blocks), key=lambda k: (-bin(k).count("1"), k))
    when = [(1, 1), (1, 2), (2, 4), (2, 5), (2, 6)]
    steps = []
    for i, (k, h) in enumerate((k, h) for k in order for h in range(HALVES)):
        for level in range(ROW_LEVELS):
            rate, first = when[level]
            steps.append((rate * i + first, -level, k, h))
    return [(k, h, -l, t) for t, l, k, h in sorted(steps, key=lambda s: (s[0], s[1]))]


def kernel(
    n_row, n_col, src, fac, out, xs, f, wb, msend, mrecv, acc, racc, tmp,
    src_sem, fac_sem, s_send, s_recv, m_send, m_recv, a_send, a_recv,
):
    row, col = lax.axis_index("row"), lax.axis_index("col")
    log_row, log_col = n_row.bit_length() - 1, n_col.bit_length() - 1
    levels, blocks, width = f.shape[0], f.shape[1], f.shape[2]
    cw = xs.shape[-1]
    pieces = n_col // blocks
    rows_out = width // pieces
    place = col // pieces
    block_of = [flip(place, k) for k in range(blocks)]

    def row_peer(level):
        return (flip(row, 1 << (level % log_row)), col)

    def col_peer(bit):
        return (row, flip(col, 1 << bit))

    def fold_bit(level):
        return (level - ROW_LEVELS) % log_col

    loads = {}
    for k in range(blocks):
        for h in range(HALVES):
            loads[k, h] = pltpu.make_async_copy(
                src.at[pl.ds(block_of[k] * width, width), pl.ds(h * cw, cw)],
                xs.at[0, k, h, pl.ds(0, width)],
                src_sem.at[k, h],
            )
            loads[k, h].start()
    fac_loads = {}
    for level in [0, levels - 1, levels - 2, 1, 2, levels - 3, 3, 4]:
        for side in range(2):
            fac_loads[level, side] = pltpu.make_async_copy(
                fac.at[level, :, side],
                f.at[level, :, :, pl.ds(side * width, width)],
                fac_sem.at[level, side],
            )
            fac_loads[level, side].start()

    barrier = pltpu.get_barrier_semaphore()
    peers = [row_peer(b) for b in range(min(log_row, ROW_LEVELS))] + [col_peer(b) for b in range(log_col)]
    for peer in peers:
        pl.semaphore_signal(barrier, inc=1, device_id=peer, device_id_type=MESH)
    pl.semaphore_wait(barrier, len(peers))

    copies = []

    def send(source, target, send_sem, recv_sem, peer):
        copy = pltpu.make_async_remote_copy(
            src_ref=source, dst_ref=target, send_sem=send_sem, recv_sem=recv_sem,
            device_id=peer, device_id_type=MESH,
        )
        copy.start()
        copies.append(copy)
        return copy

    steps = schedule(blocks)
    state = {}

    def send_state(level, k, h, source):
        state[level, k, h] = send(
            source, xs.at[level, k, h, pl.ds(width, width)],
            s_send.at[level, k, h], s_recv.at[level, k, h], row_peer(level),
        )

    for k, h, level, _ in steps:
        if level == 0:
            send_state(0, k, h, src.at[pl.ds(block_of[k] * width, width), pl.ds(h * cw, cw)])

    fold = {}
    fold[levels - 1] = send(
        fac.at[levels - 1, :, 1], mrecv.at[COL_LEVELS - 1],
        m_send.at[COL_LEVELS - 1], m_recv.at[COL_LEVELS - 1], col_peer(fold_bit(levels - 1)),
    )

    ready = set()

    def factor(level):
        if level not in ready:
            ready.add(level)
            fac_loads[level, 0].wait()
            fac_loads[level, 1].wait()

    def fold_stage(level):
        factor(level)
        factor(level - 1)
        slot = level - ROW_LEVELS
        fold[level].wait_recv()
        for j in range(blocks):
            own = f[level, j, :, :width] if level == levels - 1 else wb[slot, j]
            both = dot(own + mrecv[slot, j], f[level - 1, j])
            if slot > 0:
                wb[slot - 1, j] = both[:, :width]
                msend[slot - 1, j] = both[:, width:]
            else:
                f[level - 1, j] = both
        if slot > 0:
            fold[level - 1] = send(
                msend.at[slot - 1], mrecv.at[slot - 1],
                m_send.at[slot - 1], m_recv.at[slot - 1], col_peer(fold_bit(level - 1)),
            )

    sums = {}

    def contribute(k, h, value):
        if pieces > 1:
            tmp[...] = value
        for sub in sorted(range(pieces), key=lambda s: (-bin(s).count("1"), s)):
            q = k * pieces + sub
            if pieces > 1:
                start = pl.multiple_of((flip(col, sub) % pieces) * rows_out, rows_out)
                part = tmp[pl.ds(start, rows_out), :]
            else:
                part = value
            low = 0
            while low < log_col and not (q >> low) & 1:
                sums[q | (1 << low), h].wait_recv()
                part = part + racc[q | (1 << low), h]
                low += 1
            if q:
                acc[q, h] = part
                sums[q, h] = send(
                    acc.at[q, h], racc.at[q, h], a_send.at[q, h], a_recv.at[q, h], col_peer(low)
                )
            else:
                out[:, h * cw:(h + 1) * cw] = part

    stages = [(0, levels - 1), (5, levels - 2), (6, levels - 3)]
    for k, h, level, when in steps:
        while stages and when >= stages[0][0] and (len(stages) > 1 or level == ROW_LEVELS - 1):
            fold_stage(stages.pop(0)[1])
        factor(level)
        if level == 0:
            loads[k, h].wait()
        state[level, k, h].wait_recv()
        value = dot(f[level, block_of[k]], xs[level, k, h])
        if level < ROW_LEVELS - 1:
            xs[level + 1, k, h, :width] = value
            send_state(level + 1, k, h, xs.at[level + 1, k, h, pl.ds(0, width)])
        else:
            contribute(k, h, value)
    for copy in copies:
        copy.wait_send()


def shards(sources, level_factors):
    levels, blocks, _, width, _ = level_factors.shape
    columns = sources.shape[1]
    n_row, n_col = lax.axis_size("row"), lax.axis_size("col")
    rows_out = blocks * width // n_col
    cw = columns // HALVES
    dma = pltpu.SemaphoreType.DMA
    return pl.pallas_call(
        functools.partial(kernel, n_row, n_col),
        out_shape=jax.ShapeDtypeStruct((rows_out, columns), jnp.float32),
        in_specs=[pl.BlockSpec(memory_space=pl.ANY)] * 2,
        out_specs=pl.BlockSpec(memory_space=pltpu.VMEM),
        scratch_shapes=[
            pltpu.VMEM((ROW_LEVELS, blocks, HALVES, 2 * width, cw), jnp.float32),
            pltpu.VMEM((levels, blocks, width, 2 * width), jnp.float32),
            pltpu.VMEM((COL_LEVELS - 1, blocks, width, width), jnp.float32),
            pltpu.VMEM((COL_LEVELS - 1, blocks, width, width), jnp.float32),
            pltpu.VMEM((COL_LEVELS, blocks, width, width), jnp.float32),
            pltpu.VMEM((n_col, HALVES, rows_out, cw), jnp.float32),
            pltpu.VMEM((n_col, HALVES, rows_out, cw), jnp.float32),
            pltpu.VMEM((width, cw), jnp.float32),
            dma((blocks, HALVES)),
            dma((levels, 2)),
            dma((ROW_LEVELS, blocks, HALVES)),
            dma((ROW_LEVELS, blocks, HALVES)),
            dma((COL_LEVELS,)),
            dma((COL_LEVELS,)),
            dma((n_col, HALVES)),
            dma((n_col, HALVES)),
        ],
        compiler_params=pltpu.CompilerParams(
            collective_id=0, has_side_effects=True, vmem_limit_bytes=48 * 2**20
        ),
    )(sources, level_factors)


def solution(mesh):
    return jax.shard_map(
        shards,
        mesh=mesh,
        in_specs=(P(("row", "col"), None), P(None, ("row", "col"), None, None, None)),
        out_specs=P(("row", "col"), None),
        check_vma=False,
    )
```

```python
import functools

import jax
import jax.numpy as jnp
from jax import lax
from jax.experimental import pallas as pl
from jax.experimental.pallas import tpu as pltpu
from jax.sharding import PartitionSpec as P

ROW_LEVELS = 5
COL_LEVELS = 3
HALVES = 1
MESH = pl.DeviceIdType.MESH


def flip(index, mask):
    bit = 1
    while bit <= mask:
        if mask & bit:
            index = index + bit * (1 - 2 * ((index // bit) % 2))
        bit *= 2
    return index


def dot(a, b):
    return jnp.dot(a, b, precision=lax.Precision.HIGHEST, preferred_element_type=jnp.float32)


def schedule(blocks):
    order = sorted(range(blocks), key=lambda k: (-bin(k).count("1"), k))
    when = [(1, 1), (1, 2), (1, 3), (1, 4), (1, 5)]
    steps = []
    for i, (k, h) in enumerate((k, h) for k in order for h in range(HALVES)):
        for level in range(ROW_LEVELS):
            rate, first = when[level]
            steps.append((rate * i + first, level, k, h))
    return [(k, h, l, t) for t, l, k, h in sorted(steps, key=lambda s: (s[0], s[1]))]


def kernel(
    n_row, n_col, src, fac, out, xs, f, last, wb, msend, mrecv, acc, racc, tmp,
    src_sem, fac_sem, s_send, s_recv, m_send, m_recv, a_send, a_recv,
):
    row, col = lax.axis_index("row"), lax.axis_index("col")
    log_row, log_col = n_row.bit_length() - 1, n_col.bit_length() - 1
    levels, blocks, width = f.shape[0], f.shape[1], f.shape[3]
    cw = xs.shape[-1]
    pieces = n_col // blocks
    rows_out = width // pieces
    place = col // pieces
    block_of = [flip(place, k) for k in range(blocks)]

    def row_peer(level):
        return (flip(row, 1 << (level % log_row)), col)

    def col_peer(bit):
        return (row, flip(col, 1 << bit))

    def fold_bit(level):
        return (level - ROW_LEVELS) % log_col

    barrier = pltpu.get_barrier_semaphore()
    peers = [row_peer(b) for b in range(min(log_row, ROW_LEVELS))] + [col_peer(b) for b in range(log_col)]
    for peer in peers:
        pl.semaphore_signal(barrier, inc=1, device_id=peer, device_id_type=MESH)
    pl.semaphore_wait(barrier, len(peers))

    copies = []

    def send(source, target, send_sem, recv_sem, peer):
        copy = pltpu.make_async_remote_copy(
            src_ref=source, dst_ref=target, send_sem=send_sem, recv_sem=recv_sem,
            device_id=peer, device_id_type=MESH,
        )
        copy.start()
        copies.append(copy)
        return copy

    steps = schedule(blocks)
    state = {}

    def send_state(level, k, h, source):
        state[level, k, h] = send(
            source, xs.at[level, k, h, pl.ds(width, width)],
            s_send.at[level, k, h], s_recv.at[level, k, h], row_peer(level),
        )

    for k, h, level, _ in steps:
        if level == 0:
            send_state(0, k, h, src.at[pl.ds(block_of[k] * width, width), pl.ds(h * cw, cw)])

    fold = {}
    fold[levels - 1] = send(
        fac.at[levels - 1, :, 1], mrecv.at[COL_LEVELS - 1],
        m_send.at[COL_LEVELS - 1], m_recv.at[COL_LEVELS - 1], col_peer(fold_bit(levels - 1)),
    )

    loads = {}
    for k in range(blocks):
        for h in range(HALVES):
            loads[k, h] = pltpu.make_async_copy(
                src.at[pl.ds(block_of[k] * width, width), pl.ds(h * cw, cw)],
                xs.at[0, k, h, pl.ds(0, width)],
                src_sem.at[k, h],
            )
            loads[k, h].start()
    fac_loads = {}
    for level in [0, levels - 1, levels - 2, 1, 2, levels - 3, 3, 4]:
        fac_loads[level] = pltpu.make_async_copy(fac.at[level], f.at[level], fac_sem.at[level])
        fac_loads[level].start()

    ready = set()

    def factor(level):
        if level not in ready:
            ready.add(level)
            fac_loads[level].wait()

    def pair(level, j):
        if level == ROW_LEVELS - 1:
            return last[j]
        return jnp.concatenate([f[level, j, 0], f[level, j, 1]], axis=1)

    def fold_stage(level):
        factor(level)
        factor(level - 1)
        slot = level - ROW_LEVELS
        fold[level].wait_recv()
        for j in range(blocks):
            own = f[level, j, 0] if level == levels - 1 else wb[slot, j]
            both = dot(
                own + mrecv[slot, j],
                jnp.concatenate([f[level - 1, j, 0], f[level - 1, j, 1]], axis=1),
            )
            if slot > 0:
                wb[slot - 1, j] = both[:, :width]
                msend[slot - 1, j] = both[:, width:]
            else:
                last[j] = both
        if slot > 0:
            fold[level - 1] = send(
                msend.at[slot - 1], mrecv.at[slot - 1],
                m_send.at[slot - 1], m_recv.at[slot - 1], col_peer(fold_bit(level - 1)),
            )

    sums = {}

    def contribute(k, h, value):
        if pieces > 1:
            tmp[...] = value
        for sub in sorted(range(pieces), key=lambda s: (-bin(s).count("1"), s)):
            q = k * pieces + sub
            if pieces > 1:
                start = pl.multiple_of((flip(col, sub) % pieces) * rows_out, rows_out)
                part = tmp[pl.ds(start, rows_out), :]
            else:
                part = value
            low = 0
            while low < log_col and not (q >> low) & 1:
                sums[q | (1 << low), h].wait_recv()
                part = part + racc[q | (1 << low), h]
                low += 1
            if q:
                acc[q, h] = part
                sums[q, h] = send(
                    acc.at[q, h], racc.at[q, h], a_send.at[q, h], a_recv.at[q, h], col_peer(low)
                )
            else:
                out[:, h * cw:(h + 1) * cw] = part

    stages = [(0, levels - 1), (3, levels - 2), (4, levels - 3)]
    for k, h, level, when in steps:
        while stages and when >= stages[0][0]:
            fold_stage(stages.pop(0)[1])
        factor(level)
        if level == 0:
            loads[k, h].wait()
        state[level, k, h].wait_recv()
        value = dot(pair(level, block_of[k]), xs[level, k, h])
        if level < ROW_LEVELS - 1:
            xs[level + 1, k, h, :width] = value
            send_state(level + 1, k, h, xs.at[level + 1, k, h, pl.ds(0, width)])
        else:
            contribute(k, h, value)
    for copy in copies:
        copy.wait_send()


def shards(sources, level_factors):
    levels, blocks, _, width, _ = level_factors.shape
    columns = sources.shape[1]
    n_row, n_col = lax.axis_size("row"), lax.axis_size("col")
    rows_out = blocks * width // n_col
    cw = columns // HALVES
    dma = pltpu.SemaphoreType.DMA
    return pl.pallas_call(
        functools.partial(kernel, n_row, n_col),
        out_shape=jax.ShapeDtypeStruct((rows_out, columns), jnp.float32),
        in_specs=[pl.BlockSpec(memory_space=pltpu.HBM)] * 2,
        out_specs=pl.BlockSpec(memory_space=pltpu.VMEM),
        scratch_shapes=[
            pltpu.VMEM((ROW_LEVELS, blocks, HALVES, 2 * width, cw), jnp.float32),
            pltpu.VMEM((levels, blocks, 2, width, width), jnp.float32),
            pltpu.VMEM((blocks, width, 2 * width), jnp.float32),
            pltpu.VMEM((COL_LEVELS - 1, blocks, width, width), jnp.float32),
            pltpu.VMEM((COL_LEVELS - 1, blocks, width, width), jnp.float32),
            pltpu.VMEM((COL_LEVELS, blocks, width, width), jnp.float32),
            pltpu.VMEM((n_col, HALVES, rows_out, cw), jnp.float32),
            pltpu.VMEM((n_col, HALVES, rows_out, cw), jnp.float32),
            pltpu.VMEM((width, cw), jnp.float32),
            dma((blocks, HALVES)),
            dma((levels,)),
            dma((ROW_LEVELS, blocks, HALVES)),
            dma((ROW_LEVELS, blocks, HALVES)),
            dma((COL_LEVELS,)),
            dma((COL_LEVELS,)),
            dma((n_col, HALVES)),
            dma((n_col, HALVES)),
        ],
        compiler_params=pltpu.CompilerParams(
            collective_id=0, has_side_effects=True, vmem_limit_bytes=48 * 2**20
        ),
    )(sources, level_factors)


def solution(mesh):
    return jax.shard_map(
        shards,
        mesh=mesh,
        in_specs=(P(("row", "col"), None), P(None, ("row", "col"), None, None, None)),
        out_specs=P(("row", "col"), None),
        check_vma=False,
    )
```

```python
import functools

import jax
import jax.numpy as jnp
from jax import lax
from jax.experimental import pallas as pl
from jax.experimental.pallas import tpu as pltpu
from jax.sharding import PartitionSpec as P

ROW_LEVELS = 5
COL_LEVELS = 3
HALVES = 2
SPLIT = (True, True)
BYINDEX = True
STAGES = (0, 6)
MESH = pl.DeviceIdType.MESH


def flip(index, mask):
    bit = 1
    while bit <= mask:
        if mask & bit:
            index = index + bit * (1 - 2 * ((index // bit) % 2))
        bit *= 2
    return index


def dot(a, b):
    return jnp.dot(a, b, precision=lax.Precision.HIGHEST, preferred_element_type=jnp.float32)


def schedule(blocks):
    order = sorted(range(blocks), key=lambda k: (-bin(k).count("1"), k))
    parts = []
    for k in order:
        if SPLIT[0] and k == order[0] or SPLIT[1] and k == order[-1]:
            parts += [(k, h, 1) for h in range(HALVES)]
        else:
            parts.append((k, 0, HALVES))
    steps, end = [], 0
    for i, (k, h, n) in enumerate(parts):
        end += n / HALVES
        steps += [((i if BYINDEX else end) + level, level, k, h, n) for level in range(ROW_LEVELS)]
    return [(k, h, n, level) for _, level, k, h, n in sorted(steps, key=lambda s: s[:2])]


def kernel(
    n_row, n_col, src, fac, out, first, xs, f, last, wb, msend, mrecv, acc, racc, tmp,
    src_sem, fac_sem, s_send, s_recv, m_send, m_recv, a_send, a_recv,
):
    row, col = lax.axis_index("row"), lax.axis_index("col")
    log_row, log_col = n_row.bit_length() - 1, n_col.bit_length() - 1
    levels, blocks, width = f.shape[0], f.shape[1], f.shape[3]
    cw = xs.shape[-1]
    pieces = n_col // blocks
    rows_out = width // pieces
    place = col // pieces
    block_of = [flip(place, k) for k in range(blocks)]

    def row_peer(level):
        return (flip(row, 1 << (level % log_row)), col)

    def col_peer(bit):
        return (row, flip(col, 1 << bit))

    def fold_bit(level):
        return (level - ROW_LEVELS) % log_col

    barrier = pltpu.get_barrier_semaphore()
    peers = [row_peer(b) for b in range(min(log_row, ROW_LEVELS))] + [col_peer(b) for b in range(log_col)]
    for peer in peers:
        pl.semaphore_signal(barrier, inc=1, device_id=peer, device_id_type=MESH)
    pl.semaphore_wait(barrier, len(peers))

    copies = []

    def send(source, target, send_sem, recv_sem, peer):
        copy = pltpu.make_async_remote_copy(
            src_ref=source, dst_ref=target, send_sem=send_sem, recv_sem=recv_sem,
            device_id=peer, device_id_type=MESH,
        )
        copy.start()
        copies.append(copy)
        return copy

    steps = schedule(blocks)
    state = {}

    def send_state(level, k, h, n, source):
        if level == 0:
            target = first.at[k, pl.ds(width, width), pl.ds(h * cw, n * cw)]
        else:
            target = xs.at[level - 1, k, pl.ds(h, n), pl.ds(width, width)]
        state[level, k, h] = send(
            source, target, s_send.at[level, k, h], s_recv.at[level, k, h], row_peer(level)
        )

    for k, h, n, level in steps:
        if level == 0:
            source = src.at[pl.ds(block_of[k] * width, width), pl.ds(h * cw, n * cw)]
            send_state(0, k, h, n, source)

    fold = {}
    fold[levels - 1] = send(
        fac.at[levels - 1, :, 1], mrecv.at[COL_LEVELS - 1],
        m_send.at[COL_LEVELS - 1], m_recv.at[COL_LEVELS - 1], col_peer(fold_bit(levels - 1)),
    )

    loads = {}
    for k in range(blocks):
        loads[k] = pltpu.make_async_copy(
            src.at[pl.ds(block_of[k] * width, width)], first.at[k, pl.ds(0, width)], src_sem.at[k]
        )
        loads[k].start()
    fac_loads = {}
    for level in [0, levels - 1, levels - 2, 1, 2, levels - 3, 3, 4]:
        fac_loads[level] = pltpu.make_async_copy(fac.at[level], f.at[level], fac_sem.at[level])
        fac_loads[level].start()

    ready = set()

    def factor(level):
        if level not in ready:
            ready.add(level)
            fac_loads[level].wait()

    def pair(level, j):
        if level == ROW_LEVELS - 1:
            return last[j]
        return jnp.concatenate([f[level, j, 0], f[level, j, 1]], axis=1)

    def fold_stage(level):
        factor(level)
        factor(level - 1)
        slot = level - ROW_LEVELS
        fold[level].wait_recv()
        for j in range(blocks):
            own = f[level, j, 0] if level == levels - 1 else wb[slot, j]
            both = dot(
                own + mrecv[slot, j],
                jnp.concatenate([f[level - 1, j, 0], f[level - 1, j, 1]], axis=1),
            )
            if slot > 0:
                wb[slot - 1, j] = both[:, :width]
                msend[slot - 1, j] = both[:, width:]
            else:
                last[j] = both
        if slot > 0:
            fold[level - 1] = send(
                msend.at[slot - 1], mrecv.at[slot - 1],
                m_send.at[slot - 1], m_recv.at[slot - 1], col_peer(fold_bit(level - 1)),
            )

    def side_by_side(ref, h, n):
        return ref[h] if n == 1 else jnp.concatenate([ref[h + i] for i in range(n)], axis=1)

    def put(ref, h, n, value):
        for i in range(n):
            ref[h + i, :value.shape[0]] = value[:, i * cw:(i + 1) * cw]

    sums = {}

    def landed(q, h, n):
        for start, halves in list(sums[q]):
            if start < h + n and h < start + halves:
                copy = sums[q][start, halves]
                if copy is not None:
                    copy.wait_recv()
                sums[q][start, halves] = None
        return side_by_side(racc.at[q], h, n)

    def contribute(k, h, n, value):
        if pieces > 1:
            tmp[:, :n * cw] = value
        for sub in sorted(range(pieces), key=lambda s: (-bin(s).count("1"), s)):
            q = k * pieces + sub
            if pieces > 1:
                start = pl.multiple_of((flip(col, sub) % pieces) * rows_out, rows_out)
                part = tmp[pl.ds(start, rows_out), :n * cw]
            else:
                part = value
            low = 0
            while low < log_col and not (q >> low) & 1:
                part = part + landed(q | (1 << low), h, n)
                low += 1
            if q:
                put(acc.at[q], h, n, part)
                sums.setdefault(q, {})[h, n] = send(
                    acc.at[q, pl.ds(h, n)], racc.at[q, pl.ds(h, n)],
                    a_send.at[q, h], a_recv.at[q, h], col_peer(low),
                )
            else:
                out[:, h * cw:(h + n) * cw] = part

    stages = {STAGES[i]: levels - 1 - i for i in range(COL_LEVELS - 1)}
    folded, loaded = False, set()
    for i, (k, h, n, level) in enumerate(steps):
        if i in stages:
            fold_stage(stages[i])
        if level == ROW_LEVELS - 1 and not folded:
            fold_stage(ROW_LEVELS)
            folded = True
        factor(level)
        if level == 0 and k not in loaded:
            loads[k].wait()
            loaded.add(k)
        state[level, k, h].wait_recv()
        if level == 0:
            block = first[k, :, h * cw:(h + n) * cw]
        else:
            block = side_by_side(xs.at[level - 1, k], h, n)
        value = dot(pair(level, block_of[k]), block)
        if level < ROW_LEVELS - 1:
            put(xs.at[level, k], h, n, value)
            send_state(
                level + 1, k, h, n, xs.at[level, k, pl.ds(h, n), pl.ds(0, width)]
            )
        else:
            contribute(k, h, n, value)
    for copy in copies:
        copy.wait_send()


def shards(sources, level_factors):
    levels, blocks, _, width, _ = level_factors.shape
    columns = sources.shape[1]
    n_row, n_col = lax.axis_size("row"), lax.axis_size("col")
    rows_out = blocks * width // n_col
    cw = columns // HALVES
    dma = pltpu.SemaphoreType.DMA
    return pl.pallas_call(
        functools.partial(kernel, n_row, n_col),
        out_shape=jax.ShapeDtypeStruct((rows_out, columns), jnp.float32),
        in_specs=[pl.BlockSpec(memory_space=pltpu.HBM)] * 2,
        out_specs=pl.BlockSpec(memory_space=pltpu.VMEM),
        scratch_shapes=[
            pltpu.VMEM((blocks, 2 * width, columns), jnp.float32),
            pltpu.VMEM((ROW_LEVELS - 1, blocks, HALVES, 2 * width, cw), jnp.float32),
            pltpu.VMEM((levels, blocks, 2, width, width), jnp.float32),
            pltpu.VMEM((blocks, width, 2 * width), jnp.float32),
            pltpu.VMEM((COL_LEVELS - 1, blocks, width, width), jnp.float32),
            pltpu.VMEM((COL_LEVELS - 1, blocks, width, width), jnp.float32),
            pltpu.VMEM((COL_LEVELS, blocks, width, width), jnp.float32),
            pltpu.VMEM((n_col, HALVES, rows_out, cw), jnp.float32),
            pltpu.VMEM((n_col, HALVES, rows_out, cw), jnp.float32),
            pltpu.VMEM((width, columns), jnp.float32),
            dma((blocks,)),
            dma((levels,)),
            dma((ROW_LEVELS, blocks, HALVES)),
            dma((ROW_LEVELS, blocks, HALVES)),
            dma((COL_LEVELS,)),
            dma((COL_LEVELS,)),
            dma((n_col, HALVES)),
            dma((n_col, HALVES)),
        ],
        compiler_params=pltpu.CompilerParams(
            collective_id=0, has_side_effects=True, vmem_limit_bytes=48 * 2**20
        ),
    )(sources, level_factors)


def solution(mesh):
    return jax.shard_map(
        shards,
        mesh=mesh,
        in_specs=(P(("row", "col"), None), P(None, ("row", "col"), None, None, None)),
        out_specs=P(("row", "col"), None),
        check_vma=False,
    )
```

```python
import functools

import jax
import jax.numpy as jnp
from jax import lax
from jax.experimental import pallas as pl
from jax.experimental.pallas import tpu as pltpu
from jax.sharding import PartitionSpec as P

ROW_LEVELS = 5
COL_LEVELS = 3
HALVES = 2
SPLIT = (True, True)
STAGES = (0, 6)
MESH = pl.DeviceIdType.MESH


def flip(index, mask):
    bit = 1
    while bit <= mask:
        if mask & bit:
            index = index + bit * (1 - 2 * ((index // bit) % 2))
        bit *= 2
    return index


def dot(a, b):
    return jnp.dot(a, b, precision=lax.Precision.HIGHEST, preferred_element_type=jnp.float32)


def schedule(blocks):
    order = sorted(range(blocks), key=lambda k: (-bin(k).count("1"), k))
    parts = []
    for k in order:
        if SPLIT[0] and k == order[0] or SPLIT[1] and k == order[-1]:
            parts += [(k, h, 1) for h in range(HALVES)]
        else:
            parts.append((k, 0, HALVES))
    steps, end = [], 0
    for i, (k, h, n) in enumerate(parts):
        end += n / HALVES
        steps += [(i + 1.5 * level, level, k, h, n) for level in range(ROW_LEVELS)]
    return [(k, h, n, level) for _, level, k, h, n in sorted(steps, key=lambda s: s[:2])]


def kernel(
    n_row, n_col, src, fac, out, first, xs, f, last, wb, msend, mrecv, acc, racc, tmp,
    src_sem, fac_sem, s_send, s_recv, m_send, m_recv, a_send, a_recv,
):
    row, col = lax.axis_index("row"), lax.axis_index("col")
    log_row, log_col = n_row.bit_length() - 1, n_col.bit_length() - 1
    levels, blocks, width = f.shape[0], f.shape[1], f.shape[3]
    cw = xs.shape[-1]
    pieces = n_col // blocks
    rows_out = width // pieces
    place = col // pieces
    block_of = [flip(place, k) for k in range(blocks)]

    def row_peer(level):
        return (flip(row, 1 << (level % log_row)), col)

    def col_peer(bit):
        return (row, flip(col, 1 << bit))

    def fold_bit(level):
        return (level - ROW_LEVELS) % log_col

    barrier = pltpu.get_barrier_semaphore()
    peers = [row_peer(b) for b in range(min(log_row, ROW_LEVELS))] + [col_peer(b) for b in range(log_col)]
    for peer in peers:
        pl.semaphore_signal(barrier, inc=1, device_id=peer, device_id_type=MESH)
    pl.semaphore_wait(barrier, len(peers))

    copies = []

    def send(source, target, send_sem, recv_sem, peer):
        copy = pltpu.make_async_remote_copy(
            src_ref=source, dst_ref=target, send_sem=send_sem, recv_sem=recv_sem,
            device_id=peer, device_id_type=MESH,
        )
        copy.start()
        copies.append(copy)
        return copy

    steps = schedule(blocks)
    state = {}

    def send_state(level, k, h, n, source):
        if level == 0:
            target = first.at[k, pl.ds(width, width), pl.ds(h * cw, n * cw)]
        else:
            target = xs.at[level - 1, k, pl.ds(h, n), pl.ds(width, width)]
        state[level, k, h] = send(
            source, target, s_send.at[level, k, h], s_recv.at[level, k, h], row_peer(level)
        )

    for k, h, n, level in steps:
        if level == 0:
            source = src.at[pl.ds(block_of[k] * width, width), pl.ds(h * cw, n * cw)]
            send_state(0, k, h, n, source)

    fold = {}
    fold[levels - 1] = send(
        fac.at[levels - 1, :, 1], mrecv.at[COL_LEVELS - 1],
        m_send.at[COL_LEVELS - 1], m_recv.at[COL_LEVELS - 1], col_peer(fold_bit(levels - 1)),
    )

    loads = {}
    for k in range(blocks):
        loads[k] = pltpu.make_async_copy(
            src.at[pl.ds(block_of[k] * width, width)], first.at[k, pl.ds(0, width)], src_sem.at[k]
        )
        loads[k].start()
    fac_loads = {}
    for level in [0, levels - 1, levels - 2, 1, 2, levels - 3, 3, 4]:
        fac_loads[level] = pltpu.make_async_copy(fac.at[level], f.at[level], fac_sem.at[level])
        fac_loads[level].start()

    ready = set()

    def factor(level):
        if level not in ready:
            ready.add(level)
            fac_loads[level].wait()

    def pair(level, j):
        if level == ROW_LEVELS - 1:
            return last[j]
        return jnp.concatenate([f[level, j, 0], f[level, j, 1]], axis=1)

    def fold_stage(level):
        factor(level)
        factor(level - 1)
        slot = level - ROW_LEVELS
        fold[level].wait_recv()
        for j in range(blocks):
            own = f[level, j, 0] if level == levels - 1 else wb[slot, j]
            both = dot(
                own + mrecv[slot, j],
                jnp.concatenate([f[level - 1, j, 0], f[level - 1, j, 1]], axis=1),
            )
            if slot > 0:
                wb[slot - 1, j] = both[:, :width]
                msend[slot - 1, j] = both[:, width:]
            else:
                last[j] = both
        if slot > 0:
            fold[level - 1] = send(
                msend.at[slot - 1], mrecv.at[slot - 1],
                m_send.at[slot - 1], m_recv.at[slot - 1], col_peer(fold_bit(level - 1)),
            )

    def side_by_side(ref, h, n):
        return ref[h] if n == 1 else jnp.concatenate([ref[h + i] for i in range(n)], axis=1)

    def put(ref, h, n, value):
        for i in range(n):
            ref[h + i, :value.shape[0]] = value[:, i * cw:(i + 1) * cw]

    sums = {}

    def landed(q, h, n):
        for start, halves in list(sums[q]):
            if start < h + n and h < start + halves:
                copy = sums[q][start, halves]
                if copy is not None:
                    copy.wait_recv()
                sums[q][start, halves] = None
        return side_by_side(racc.at[q], h, n)

    def contribute(k, h, n, value):
        if pieces > 1:
            tmp[:, :n * cw] = value
        for sub in sorted(range(pieces), key=lambda s: (-bin(s).count("1"), s)):
            q = k * pieces + sub
            if pieces > 1:
                start = pl.multiple_of((flip(col, sub) % pieces) * rows_out, rows_out)
                part = tmp[pl.ds(start, rows_out), :n * cw]
            else:
                part = value
            low = 0
            while low < log_col and not (q >> low) & 1:
                part = part + landed(q | (1 << low), h, n)
                low += 1
            if q:
                put(acc.at[q], h, n, part)
                sums.setdefault(q, {})[h, n] = send(
                    acc.at[q, pl.ds(h, n)], racc.at[q, pl.ds(h, n)],
                    a_send.at[q, h], a_recv.at[q, h], col_peer(low),
                )
            else:
                out[:, h * cw:(h + n) * cw] = part

    stages = {STAGES[i]: levels - 1 - i for i in range(COL_LEVELS - 1)}
    folded, loaded = False, set()
    for i, (k, h, n, level) in enumerate(steps):
        if i in stages:
            fold_stage(stages[i])
        if level == ROW_LEVELS - 1 and not folded:
            fold_stage(ROW_LEVELS)
            folded = True
        factor(level)
        if level == 0 and k not in loaded:
            loads[k].wait()
            loaded.add(k)
        state[level, k, h].wait_recv()
        if level == 0:
            block = first[k, :, h * cw:(h + n) * cw]
        else:
            block = side_by_side(xs.at[level - 1, k], h, n)
        value = dot(pair(level, block_of[k]), block)
        if level < ROW_LEVELS - 1:
            put(xs.at[level, k], h, n, value)
            send_state(
                level + 1, k, h, n, xs.at[level, k, pl.ds(h, n), pl.ds(0, width)]
            )
        else:
            contribute(k, h, n, value)
    for copy in copies:
        copy.wait_send()


def shards(sources, level_factors):
    levels, blocks, _, width, _ = level_factors.shape
    columns = sources.shape[1]
    n_row, n_col = lax.axis_size("row"), lax.axis_size("col")
    rows_out = blocks * width // n_col
    cw = columns // HALVES
    dma = pltpu.SemaphoreType.DMA
    return pl.pallas_call(
        functools.partial(kernel, n_row, n_col),
        out_shape=jax.ShapeDtypeStruct((rows_out, columns), jnp.float32),
        in_specs=[pl.BlockSpec(memory_space=pltpu.HBM)] * 2,
        out_specs=pl.BlockSpec(memory_space=pltpu.VMEM),
        scratch_shapes=[
            pltpu.VMEM((blocks, 2 * width, columns), jnp.float32),
            pltpu.VMEM((ROW_LEVELS - 1, blocks, HALVES, 2 * width, cw), jnp.float32),
            pltpu.VMEM((levels, blocks, 2, width, width), jnp.float32),
            pltpu.VMEM((blocks, width, 2 * width), jnp.float32),
            pltpu.VMEM((COL_LEVELS - 1, blocks, width, width), jnp.float32),
            pltpu.VMEM((COL_LEVELS - 1, blocks, width, width), jnp.float32),
            pltpu.VMEM((COL_LEVELS, blocks, width, width), jnp.float32),
            pltpu.VMEM((n_col, HALVES, rows_out, cw), jnp.float32),
            pltpu.VMEM((n_col, HALVES, rows_out, cw), jnp.float32),
            pltpu.VMEM((width, columns), jnp.float32),
            dma((blocks,)),
            dma((levels,)),
            dma((ROW_LEVELS, blocks, HALVES)),
            dma((ROW_LEVELS, blocks, HALVES)),
            dma((COL_LEVELS,)),
            dma((COL_LEVELS,)),
            dma((n_col, HALVES)),
            dma((n_col, HALVES)),
        ],
        compiler_params=pltpu.CompilerParams(
            collective_id=0, has_side_effects=True, vmem_limit_bytes=48 * 2**20
        ),
    )(sources, level_factors)


def solution(mesh):
    return jax.shard_map(
        shards,
        mesh=mesh,
        in_specs=(P(("row", "col"), None), P(None, ("row", "col"), None, None, None)),
        out_specs=P(("row", "col"), None),
        check_vma=False,
    )
```
